256 devices in a mesh: angle: 8 (over x_hi, y), tile: 16 (over z, core), layer: 2 (over x_lo).
Axes of the slice: x: 4 (x_hi: 2, x_lo: 2; x = x_hi * 2 + x_lo), y: 4, z: 8, core: 2. Of those that a mesh axis runs over, the one named last changes fastest.
Arguments:
- frames: bfloat16 [2, 1024, 384, 2048], P('layer', 'angle', 'tile'), may hold values from 0.0625 to 8, as said below
- exponents: int32 [2, 1024, 384, 16], P('layer', 'angle', 'tile'), may hold values from -1 to 1
- valid_mask: int32 [2, 384, 2048], P('layer', 'tile', 'angle'), may hold values 0 or 1
Outputs:
- orientation: float32 [2, 2, 384, 2048], P(None, 'layer', 'tile', 'angle')
- spread: float32 [3, 2, 384, 2048], P(None, 'layer', 'tile', 'angle')
- nye_tensor: float32 [7, 2, 384, 2048], P(None, 'layer', 'tile', 'angle')
The draws below stay inside these ranges and needn't reach their ends.
Inputs may be any that keep to these rules, and one draw needn't show every extreme that they name: `frames`: positive intensities.
All inputs are finite; a program needn't handle non-finite values. No bound on the sum of `valid_mask` on one device may be relied on, other than what follows from the above.
Results may differ from the reference program's by a relative error of at most 0.0003.
Values sent between devices are 32-bit elements; how exact they have to be, the bound alone decides.
A program may use at most 128 MiB of HBM per device.

```python
import math
import jax
import jax.numpy as jnp
from jax import lax

NPHI = 32
NCHI = 32
QBLK = 128
ROWS_DEV = 24
ANGLES = 1024
LAYERS = 2
ROWS = 384
COLS = 2048


def draw_frames(key, part):
    subkeys = jax.random.split(jax.random.fold_in(key, 17), 5)
    pixel_shape = (LAYERS, 1, ROWS, COLS)
    position = jnp.arange(ANGLES, dtype=jnp.int32)
    phi_coord = ((position // NCHI).astype(jnp.float32) - 0.5 * (NPHI - 1)) / (0.5 * NPHI)
    chi_coord = ((position % NCHI).astype(jnp.float32) - 0.5 * (NCHI - 1)) / (0.5 * NCHI)
    phi_coord = phi_coord.reshape(1, ANGLES, 1, 1)
    chi_coord = chi_coord.reshape(1, ANGLES, 1, 1)
    extent = 0.6
    narrowest = 0.12
    broadest = 0.4
    height = jnp.exp(jax.random.uniform(subkeys[2], pixel_shape, minval=math.log(2.0), maxval=math.log(40.0)))
    centre_phi = jax.random.uniform(subkeys[0], pixel_shape, minval=-extent, maxval=extent)
    centre_chi = jax.random.uniform(subkeys[1], pixel_shape, minval=-extent, maxval=extent)
    breadth = jnp.exp(jax.random.uniform(subkeys[3], pixel_shape, minval=math.log(narrowest), maxval=math.log(broadest)))
    distance = (phi_coord - centre_phi) ** 2 + (chi_coord - centre_chi) ** 2
    profile = height * jnp.exp(-distance / (2.0 * breadth * breadth))
    jitter = jax.random.uniform(subkeys[4], (LAYERS, ANGLES, ROWS, COLS))
    result = profile * (0.7 + 0.6 * jitter) + 0.05 + 0.25 * (1.0 - jitter)
    return jnp.clip(result, 0.0625, 8.0).astype(jnp.bfloat16)


def touch_ends(values, own_key, least, largest):
    longest = values.shape.index(max(values.shape))
    spots = []
    for shift in (0, 1):
        where = [jax.random.randint(jax.random.fold_in(own_key, axis), (), 0, length) for axis, length in enumerate(values.shape)]
        where[longest] = (where[longest] + shift) % values.shape[longest]
        spots.append(tuple(where))
    return values.at[spots[0]].set(least).at[spots[1]].set(largest)


def setup_inputs(seed: int = 0) -> dict:
    streams_of = jax.random.split(jax.random.key(seed), 4)
    return {
        "frames": draw_frames(jax.random.fold_in(streams_of[3], 71), 0),
        "exponents": touch_ends(jax.random.randint(streams_of[1], (LAYERS, ANGLES, ROWS, COLS // QBLK), -1, 2), jax.random.fold_in(streams_of[1], 1), -1, 1).astype(jnp.int32),
        "valid_mask": touch_ends((jax.random.randint(streams_of[2], (LAYERS, ROWS, COLS), 0, 8) < 7).astype(jnp.int32), jax.random.fold_in(streams_of[2], 1), 0, 1),
    }


layer_pitch = 2.0


def angle_table(first_angle, count_angles):
    position = first_angle + jnp.arange(count_angles, dtype=jnp.int32)
    phi_index = (position // NCHI).astype(jnp.float32)
    chi_index = (position % NCHI).astype(jnp.float32)
    phi_coord = (phi_index - 0.5 * (NPHI - 1)) / (0.5 * NPHI)
    chi_coord = (chi_index - 0.5 * (NCHI - 1)) / (0.5 * NCHI)
    constant = jnp.ones_like(phi_coord)
    return jnp.stack([constant, phi_coord, chi_coord, phi_coord * phi_coord,
                      chi_coord * chi_coord, phi_coord * chi_coord]).astype(jnp.bfloat16)


def intensity_of(frames, exponents):
    layers_here, angles_here, rows_here, columns = frames.shape
    blocks = exponents.shape[3]
    factor = jnp.exp2(exponents.astype(jnp.float32)).astype(jnp.bfloat16)
    scaled = frames.reshape(layers_here, angles_here, rows_here, blocks, columns // blocks) * factor[..., None]
    return scaled.reshape(layers_here, angles_here, rows_here * columns)


def orientation_of(moments):
    zeroth = moments[0]
    return jnp.stack([moments[1] / zeroth, moments[2] / zeroth])


def spread_of(moments, orient):
    zeroth = moments[0]
    return jnp.stack([moments[3] / zeroth - orient[0] * orient[0],
                      moments[4] / zeroth - orient[1] * orient[1],
                      moments[5] / zeroth - orient[0] * orient[1]])


def nye_of(padded):
    along_x = 0.5 * (padded[:, 1:-1, 1:-1, 2:] - padded[:, 1:-1, 1:-1, :-2])
    along_y = 0.5 * (padded[:, 1:-1, 2:, 1:-1] - padded[:, 1:-1, :-2, 1:-1])
    along_z = (0.5 / layer_pitch) * (padded[:, 2:, 1:-1, 1:-1] - padded[:, :-2, 1:-1, 1:-1])
    trace_sum = along_x[0] + along_y[1]
    return jnp.stack([-along_y[1], -along_x[0], -trace_sum, along_x[1], along_y[0], along_z[0], along_z[1]])


def reference(frames, exponents, valid_mask):
    layers, angles, rows_all, columns = frames.shape
    blocks = exponents.shape[3]
    angle_weights = angle_table(jnp.zeros((), jnp.int32), angles)
    row_block = ROWS_DEV
    row_blocks = rows_all // row_block

    def one_piece(item_index):
        layer_index = item_index // row_blocks
        first_row = (item_index % row_blocks) * row_block
        anchor = jnp.zeros((), jnp.int32)
        frame_piece = lax.dynamic_slice(frames, (layer_index, anchor, first_row, anchor),
                                        (1, angles, row_block, columns))
        scale_piece = lax.dynamic_slice(exponents, (layer_index, anchor, first_row, anchor),
                                        (1, angles, row_block, blocks))
        intensity = intensity_of(frame_piece, scale_piece)[0]
        return jnp.dot(angle_weights, intensity, preferred_element_type=jnp.float32).reshape(6, row_block, columns)

    stacked = lax.map(one_piece, jnp.arange(layers * row_blocks, dtype=jnp.int32))
    moments = stacked.reshape(layers, row_blocks, 6, row_block, columns)
    moments = moments.transpose(2, 0, 1, 3, 4).reshape(6, layers, rows_all, columns)
    orient = orientation_of(moments)
    mask_float = valid_mask.astype(jnp.float32)
    spread = spread_of(moments, orient) * mask_float
    padded = jnp.pad(orient, ((0, 0), (1, 1), (1, 1), (1, 1)))
    nye_tensor = nye_of(padded) * mask_float
    return orient * mask_float, spread, nye_tensor
```

```python
import functools

import jax
import jax.numpy as jnp
from jax import lax
from jax.experimental import pallas as pl
from jax.experimental.pallas import tpu as pltpu
from jax.sharding import PartitionSpec as P

NPHI = 32
NCHI = 32
MOMENTS = 6
ROWS = 24
ANGLES_HERE = 128
LANES = 128
HALF = ANGLES_HERE // 2
DEPTH = HALF * 16
LAYER_PITCH = 2.0
MESH = pl.DeviceIdType.MESH


def fill_tables(me, spread_ref, weight_ref):
    lane = lax.broadcasted_iota(jnp.int32, (ANGLES_HERE, DEPTH), 1)
    source = lax.broadcasted_iota(jnp.int32, (ANGLES_HERE, DEPTH), 0)
    pair = lane >> 4
    for parity in range(2):
        hit = source == 2 * pair + parity
        spread_ref[parity * ANGLES_HERE : (parity + 1) * ANGLES_HERE, :] = jnp.where(
            hit, 1.0, 0.0
        ).astype(jnp.bfloat16)
    lane = lax.broadcasted_iota(jnp.int32, (16, DEPTH), 1)
    row = lax.broadcasted_iota(jnp.int32, (16, DEPTH), 0)
    inner = lane & 15
    keep = inner == row
    for kind in range(3):
        if kind == 0:
            parity = 0
        elif kind == 2:
            parity = 1
        else:
            parity = inner >> 3
        angle = me * ANGLES_HERE + 2 * (lane >> 4) + parity
        phi = ((angle >> 5).astype(jnp.float32) - 0.5 * (NPHI - 1)) / (0.5 * NPHI)
        chi = ((angle & 31).astype(jnp.float32) - 0.5 * (NCHI - 1)) / (0.5 * NCHI)
        rows = (jnp.ones_like(phi), phi, chi, phi * phi, chi * chi, phi * chi)
        for m in range(MOMENTS):
            weight_ref[kind, m] = jnp.where(keep, rows[m], 0.0).astype(jnp.bfloat16)


def fill_factors(exp_ref, factor_ref):
    blank = jnp.zeros((8, ANGLES_HERE), jnp.float32)

    def one(k, carry):
        code = exp_ref[pl.ds(k, ROWS, stride=16), :]
        factor = jnp.exp2(code.astype(jnp.float32))
        low, mid, high = factor[0:8], factor[8:16], factor[16:24]
        even = jnp.concatenate([low, mid, high, blank, blank, blank], axis=0)
        odd = jnp.concatenate([blank, blank, blank, low, mid, high], axis=0)
        both = jnp.concatenate([even, odd], axis=1)
        factor_ref[k] = both.astype(jnp.bfloat16)
        return carry

    lax.fori_loop(0, 16, one, 0)


def partial_moments(dest, slot, buf, factor_ref, spread_ref, weight_ref, out_ref):
    for side in range(2):
        grown = jnp.dot(
            factor_ref[2 * dest + side], spread_ref[...], preferred_element_type=jnp.float32
        ).astype(jnp.bfloat16)
        sums = []
        for kind in range(3):
            left = (
                weight_ref[kind] * grown[kind * 16 : kind * 16 + 16][None]
            ).reshape(MOMENTS * 16, DEPTH)
            right = buf[
                slot, :, kind * 16 : kind * 16 + 16, side * LANES : (side + 1) * LANES
            ].reshape(DEPTH, LANES)
            sums.append(
                jnp.dot(left, right, preferred_element_type=jnp.float32).reshape(
                    MOMENTS, 16, LANES
                )
            )
        first, second, third = sums
        here = slice(side * LANES, (side + 1) * LANES)
        out_ref[slot, :, 0:8, here] = first[:, 0:8] + second[:, 8:16]
        out_ref[slot, :, 8:16, here] = first[:, 8:16] + third[:, 0:8]
        out_ref[slot, :, 16:24, here] = second[:, 0:8] + third[:, 8:16]


def kernel(
    count, tiles, frames, exponents, valid,
    orient_out, spread_out, nye_out,
    buf, exp_ref, mask_ref, factor_ref, spread_ref, weight_ref,
    send, recv, orient, left_halo, right_halo, up_halo, down_halo, layer_halo,
    in_sem, small_sem, send_sem, recv_sem, halo_send, halo_recv,
):
    me = lax.axis_index("angle")
    tile = lax.axis_index("tile")
    layer = lax.axis_index("layer")
    cols = 2 * LANES

    exp_copy = pltpu.make_async_copy(exponents, exp_ref, small_sem.at[0])
    exp_copy.start()

    def chunk(step):
        dest = lax.rem(me + 1 + step, count)
        begin = pl.multiple_of(dest * cols, cols)
        return pltpu.make_async_copy(
            frames.at[:, :, pl.ds(begin, cols)], buf.at[step], in_sem.at[step]
        )

    for step in range(count):
        chunk(step).start()
    mask_copy = pltpu.make_async_copy(valid, mask_ref, small_sem.at[1])
    mask_copy.start()

    barrier = pltpu.get_barrier_semaphore()
    for step in range(count - 1):
        pl.semaphore_signal(
            barrier, inc=1, device_id={"angle": lax.rem(me + 1 + step, count)},
            device_id_type=MESH,
        )
    pl.semaphore_signal(barrier, inc=1, device_id={"layer": 1 - layer}, device_id_type=MESH)

    @pl.when(tile > 0)
    def _():
        pl.semaphore_signal(barrier, inc=1, device_id={"tile": tile - 1}, device_id_type=MESH)

    @pl.when(tile < tiles - 1)
    def _():
        pl.semaphore_signal(barrier, inc=1, device_id={"tile": tile + 1}, device_id_type=MESH)

    fill_tables(me, spread_ref, weight_ref)
    exp_copy.wait()
    fill_factors(exp_ref, factor_ref)

    near = (tile > 0).astype(jnp.int32) + (tile < tiles - 1).astype(jnp.int32)
    pl.semaphore_wait(barrier, count + near)

    def remote(step):
        return pltpu.make_async_remote_copy(
            src_ref=send.at[step],
            dst_ref=recv.at[step],
            send_sem=send_sem.at[step],
            recv_sem=recv_sem.at[step],
            device_id={"angle": lax.rem(me + 1 + step, count)},
            device_id_type=MESH,
        )

    def one(step, carry):
        chunk(step).wait()
        partial_moments(
            lax.rem(me + 1 + step, count), step, buf, factor_ref, spread_ref, weight_ref, send
        )

        @pl.when(step < count - 1)
        def _():
            remote(step).start()

        return carry

    lax.fori_loop(0, count, one, 0)

    total = send[count - 1]
    for step in range(count - 1):
        remote(step).wait_recv()
        total = total + recv[step]

    field = [total[1] / total[0], total[2] / total[0]]
    orient[0] = field[0]
    orient[1] = field[1]

    def halo(index, src, dst, where):
        return pltpu.make_async_remote_copy(
            src_ref=src, dst_ref=dst, send_sem=halo_send.at[index],
            recv_sem=halo_recv.at[index], device_id=where, device_id_type=MESH,
        )

    to_layer = halo(0, orient, layer_halo, {"layer": 1 - layer})
    to_next_tile = halo(1, orient.at[:, 16:24, :], up_halo, {"tile": tile + 1})
    to_last_tile = halo(2, orient.at[:, 0:8, :], down_halo, {"tile": tile - 1})
    to_next_angle = halo(3, orient.at[:, :, LANES:cols], left_halo, {"angle": me + 1})
    to_last_angle = halo(4, orient.at[:, :, 0:LANES], right_halo, {"angle": me - 1})
    has_next_tile = tile < tiles - 1
    has_last_tile = tile > 0
    has_next_angle = me < count - 1
    has_last_angle = me > 0
    to_layer.start()
    pl.when(has_next_tile)(lambda: to_next_tile.start())
    pl.when(has_last_tile)(lambda: to_last_tile.start())
    pl.when(has_next_angle)(lambda: to_next_angle.start())
    pl.when(has_last_angle)(lambda: to_last_angle.start())

    @pl.when(jnp.logical_not(has_last_tile))
    def _():
        up_halo[...] = jnp.zeros_like(up_halo)

    @pl.when(jnp.logical_not(has_next_tile))
    def _():
        down_halo[...] = jnp.zeros_like(down_halo)

    @pl.when(jnp.logical_not(has_last_angle))
    def _():
        left_halo[...] = jnp.zeros_like(left_halo)

    @pl.when(jnp.logical_not(has_next_angle))
    def _():
        right_halo[...] = jnp.zeros_like(right_halo)

    mask_copy.wait()
    mask = mask_ref[...].astype(jnp.float32)
    orient_out[0] = field[0] * mask
    orient_out[1] = field[1] * mask
    spread_out[0] = (total[3] / total[0] - field[0] * field[0]) * mask
    spread_out[1] = (total[4] / total[0] - field[1] * field[1]) * mask
    spread_out[2] = (total[5] / total[0] - field[0] * field[1]) * mask

    pl.when(has_last_tile)(lambda: to_next_tile.wait_recv())
    pl.when(has_next_tile)(lambda: to_last_tile.wait_recv())
    pl.when(has_last_angle)(lambda: to_next_angle.wait_recv())
    pl.when(has_next_angle)(lambda: to_last_angle.wait_recv())

    lane = lax.broadcasted_iota(jnp.int32, (ROWS, cols), 1)
    row = lax.broadcasted_iota(jnp.int32, (ROWS, cols), 0)
    along_x, along_y = [], []
    for f in range(2):
        after = jnp.where(
            lane == cols - 1, right_halo[f, :, 0:1], pltpu.roll(field[f], cols - 1, 1)
        )
        before = jnp.where(
            lane == 0, left_halo[f, :, LANES - 1 : LANES], pltpu.roll(field[f], 1, 1)
        )
        along_x.append(0.5 * (after - before))
        after = jnp.where(row == ROWS - 1, down_halo[f, 0:1, :], pltpu.roll(field[f], ROWS - 1, 0))
        before = jnp.where(row == 0, up_halo[f, 7:8, :], pltpu.roll(field[f], 1, 0))
        along_y.append(0.5 * (after - before))
    nye_out[0] = -along_y[1] * mask
    nye_out[1] = -along_x[0] * mask
    nye_out[2] = -(along_x[0] + along_y[1]) * mask
    nye_out[3] = along_x[1] * mask
    nye_out[4] = along_y[0] * mask
    to_layer.wait_recv()
    slope = (0.5 / LAYER_PITCH) * (1 - 2 * layer).astype(jnp.float32) * mask
    nye_out[5] = layer_halo[0] * slope
    nye_out[6] = layer_halo[1] * slope

    for step in range(count - 1):
        remote(step).wait_send()
    to_layer.wait_send()
    pl.when(has_next_tile)(lambda: to_next_tile.wait_send())
    pl.when(has_last_tile)(lambda: to_last_tile.wait_send())
    pl.when(has_next_angle)(lambda: to_next_angle.wait_send())
    pl.when(has_last_angle)(lambda: to_last_angle.wait_send())


def on_device(count, tiles, frames, exponents, valid_mask):
    columns = frames.shape[3]
    cols = columns // count
    stack = frames.reshape(HALF, 2 * ROWS, columns)
    codes = exponents[0].transpose(1, 2, 0).reshape(ROWS * 16, ANGLES_HERE)
    f32 = jnp.float32
    bf16 = jnp.bfloat16
    anywhere = pl.BlockSpec(memory_space=pl.ANY)
    vmem = pl.BlockSpec(memory_space=pltpu.VMEM)
    out = pl.pallas_call(
        functools.partial(kernel, count, tiles),
        out_shape=[
            jax.ShapeDtypeStruct((2, ROWS, cols), f32),
            jax.ShapeDtypeStruct((3, ROWS, cols), f32),
            jax.ShapeDtypeStruct((7, ROWS, cols), f32),
        ],
        in_specs=[anywhere] * 3,
        out_specs=[vmem] * 3,
        scratch_shapes=[
            pltpu.VMEM((count, HALF, 2 * ROWS, cols), bf16),
            pltpu.VMEM((ROWS * 16, ANGLES_HERE), jnp.int32),
            pltpu.VMEM((ROWS, cols), jnp.int32),
            pltpu.VMEM((16, 48, 2 * ANGLES_HERE), bf16),
            pltpu.VMEM((2 * ANGLES_HERE, DEPTH), bf16),
            pltpu.VMEM((3, MOMENTS, 16, DEPTH), bf16),
            pltpu.VMEM((count, MOMENTS, ROWS, cols), f32),
            pltpu.VMEM((count - 1, MOMENTS, ROWS, cols), f32),
            pltpu.VMEM((2, ROWS, cols), f32),
            pltpu.VMEM((2, ROWS, LANES), f32),
            pltpu.VMEM((2, ROWS, LANES), f32),
            pltpu.VMEM((2, 8, cols), f32),
            pltpu.VMEM((2, 8, cols), f32),
            pltpu.VMEM((2, ROWS, cols), f32),
            pltpu.SemaphoreType.DMA((count,)),
            pltpu.SemaphoreType.DMA((2,)),
            pltpu.SemaphoreType.DMA((count - 1,)),
            pltpu.SemaphoreType.DMA((count - 1,)),
            pltpu.SemaphoreType.DMA((5,)),
            pltpu.SemaphoreType.DMA((5,)),
        ],
        compiler_params=pltpu.CompilerParams(
            collective_id=0, has_side_effects=True, vmem_limit_bytes=60 * 1024 * 1024
        ),
    )(stack, codes, valid_mask[0])
    return tuple(part[:, None] for part in out)


def solution(mesh):
    in_specs = (
        P("layer", "angle", "tile", None),
        P("layer", "angle", "tile", None),
        P("layer", "tile", "angle"),
    )
    out_specs = (
        P(None, "layer", "tile", "angle"),
        P(None, "layer", "tile", "angle"),
        P(None, "layer", "tile", "angle"),
    )
    return jax.shard_map(
        functools.partial(on_device, mesh.shape["angle"], mesh.shape["tile"]),
        mesh=mesh, in_specs=in_specs, out_specs=out_specs, check_vma=False,
    )
```

```python
import functools

import jax
import jax.numpy as jnp
from jax import lax
from jax.experimental import pallas as pl
from jax.experimental.pallas import tpu as pltpu
from jax.sharding import PartitionSpec as P

NPHI = 32
NCHI = 32
MOMENTS = 6
ROWS = 24
ANGLES_HERE = 128
LANES = 128
HALF = ANGLES_HERE // 2
DEPTH = HALF * 16
LAYER_PITCH = 2.0
AHEAD = 3
ORDER = (0, 2, 1)
MESH = pl.DeviceIdType.MESH


def fill_tables(me, spread_ref, weight_ref):
    lane = lax.broadcasted_iota(jnp.int32, (ANGLES_HERE, DEPTH), 1)
    source = lax.broadcasted_iota(jnp.int32, (ANGLES_HERE, DEPTH), 0)
    pair = lane >> 4
    for parity in range(2):
        hit = source == 2 * pair + parity
        spread_ref[parity * ANGLES_HERE : (parity + 1) * ANGLES_HERE, :] = jnp.where(
            hit, 1.0, 0.0
        ).astype(jnp.bfloat16)
    lane = lax.broadcasted_iota(jnp.int32, (16, DEPTH), 1)
    row = lax.broadcasted_iota(jnp.int32, (16, DEPTH), 0)
    inner = lane & 15
    keep = inner == row
    for kind in range(3):
        if kind == 0:
            parity = 0
        elif kind == 2:
            parity = 1
        else:
            parity = inner >> 3
        angle = me * ANGLES_HERE + 2 * (lane >> 4) + parity
        phi = ((angle >> 5).astype(jnp.float32) - 0.5 * (NPHI - 1)) / (0.5 * NPHI)
        chi = ((angle & 31).astype(jnp.float32) - 0.5 * (NCHI - 1)) / (0.5 * NCHI)
        rows = (jnp.ones_like(phi), phi, chi, phi * phi, chi * chi, phi * chi)
        for m in range(MOMENTS):
            weight_ref[kind, m] = jnp.where(keep, rows[m], 0.0).astype(jnp.bfloat16)


def fill_factors(exp_ref, factor_ref):
    blank = jnp.zeros((8, ANGLES_HERE), jnp.float32)

    def one(k, carry):
        code = exp_ref[pl.ds(k, ROWS, stride=16), :]
        factor = jnp.exp2(code.astype(jnp.float32))
        low, mid, high = factor[0:8], factor[8:16], factor[16:24]
        even = jnp.concatenate([low, mid, high, blank, blank, blank], axis=0)
        odd = jnp.concatenate([blank, blank, blank, low, mid, high], axis=0)
        both = jnp.concatenate([even, odd], axis=1)
        factor_ref[k] = both.astype(jnp.bfloat16)
        return carry

    lax.fori_loop(0, 16, one, 0)


def grow(role, dest, factor_ref, spread_ref, grown_ref):
    both = factor_ref[pl.ds(2 * dest, 2)].reshape(96, 2 * ANGLES_HERE)
    grown_ref[lax.rem(role, 2)] = jnp.dot(
        both, spread_ref[...], preferred_element_type=jnp.float32
    ).astype(jnp.bfloat16)


def partial_moments(role, buf, grown_ref, weight_ref, part):
    slot = lax.rem(role, 2)
    for side in range(2):
        sums = []
        for kind in range(3):
            begin = side * 48 + kind * 16
            left = (weight_ref[kind] * grown_ref[slot, begin : begin + 16][None]).reshape(
                MOMENTS * 16, DEPTH
            )
            right = buf[
                role, :, kind * 16 : kind * 16 + 16, side * LANES : (side + 1) * LANES
            ].reshape(DEPTH, LANES)
            sums.append(
                jnp.dot(left, right, preferred_element_type=jnp.float32).reshape(
                    MOMENTS, 16, LANES
                )
            )
        first, second, third = sums
        here = slice(side * LANES, (side + 1) * LANES)
        part[role, :, 0:8, here] = first[:, 0:8] + second[:, 8:16]
        part[role, :, 8:16, here] = first[:, 8:16] + third[:, 0:8]
        part[role, :, 16:24, here] = second[:, 0:8] + third[:, 8:16]


def kernel(
    sizes, frames, exponents, valid, out,
    buf, exp_ref, mask_ref, factor_ref, spread_ref, weight_ref, grown_ref,
    part, early, halves, late, last, orient,
    left_halo, right_halo, up_halo, down_halo, layer_halo,
    in_sem, small_sem, early_send, early_recv, half_send, half_recv,
    late_send, late_recv, last_send, last_recv, halo_send, halo_recv,
):
    count, tiles = sizes
    ring = count // 2
    me = lax.axis_index("angle")
    tile = lax.axis_index("tile")
    layer = lax.axis_index("layer")
    cols = 2 * LANES
    px, py = me // ring, lax.rem(me, ring)
    other = (1 - px) * ring + py
    above = px * ring + lax.rem(py + 1, ring)
    below = px * ring + lax.rem(py + ring - 1, ring)
    has_next_tile = tile < tiles - 1
    has_last_tile = tile > 0
    has_next_angle = me < count - 1
    has_last_angle = me > 0
    far_next = me == ring - 1
    far_last = me == ring

    def owner(role):
        swap = jnp.logical_or(role < 3, role == 6)
        shift = jnp.where(role >= 6, 0, 2)
        turn = lax.rem(role, 3)
        shift = jnp.where(role < 6, jnp.where(turn == 0, 2, jnp.where(turn == 1, 1, ring - 1)), 0)
        return jnp.where(swap, 1 - px, px) * ring + lax.rem(py + shift, ring)

    def chunk(role):
        begin = pl.multiple_of(owner(role) * cols, cols)
        return pltpu.make_async_copy(
            frames.at[:, :, pl.ds(begin, cols)], buf.at[role], in_sem.at[role]
        )

    exp_copy = pltpu.make_async_copy(exponents, exp_ref, small_sem.at[0])
    mask_copy = pltpu.make_async_copy(valid, mask_ref, small_sem.at[1])
    exp_copy.start()
    for role in range(AHEAD):
        chunk(jnp.int32(role)).start()

    barrier = pltpu.get_barrier_semaphore()

    def greet(where):
        pl.semaphore_signal(barrier, inc=1, device_id=where, device_id_type=MESH)

    greet({"angle": other})
    greet({"angle": above})
    greet({"angle": below})
    greet({"layer": 1 - layer})
    pl.when(has_last_tile)(lambda: greet({"tile": tile - 1}))
    pl.when(has_next_tile)(lambda: greet({"tile": tile + 1}))
    pl.when(far_next)(lambda: greet({"angle": me + 1}))
    pl.when(far_last)(lambda: greet({"angle": me - 1}))
    partners = 4
    for present in (has_last_tile, has_next_tile, far_next, far_last):
        partners = partners + present.astype(jnp.int32)

    fill_tables(me, spread_ref, weight_ref)
    exp_copy.wait()
    mask_copy.start()
    fill_factors(exp_ref, factor_ref)
    grow(jnp.int32(0), owner(jnp.int32(0)), factor_ref, spread_ref, grown_ref)

    def remote(src, dst, send, recv, where):
        return pltpu.make_async_remote_copy(
            src_ref=src, dst_ref=dst, send_sem=send, recv_sem=recv, device_id=where,
            device_id_type=MESH,
        )

    def rows(g):
        return pl.ds(8 * g, 8)

    def early_copy(role, g):
        to = jnp.where(role == 0, other, jnp.where(role == 1, above, below))
        return remote(
            part.at[role, :, rows(g), :], early.at[role, :, rows(g), :],
            early_send.at[role, g], early_recv.at[role, g], {"angle": to},
        )

    def half_copy(side, g):
        which = pl.ds(3 * side, 3)
        return remote(
            part.at[3, which, rows(g), :], halves.at[side, :, rows(g), :],
            half_send.at[side, g], half_recv.at[side, g],
            {"angle": below if side else above},
        )

    def late_copy(side, g):
        return remote(
            part.at[4 + side, :, rows(g), :], late.at[side, :, rows(g), :],
            late_send.at[side, g], late_recv.at[side, g],
            {"angle": below if side else above},
        )

    def last_copy(g):
        return remote(
            part.at[6, :, rows(g), :], last.at[:, rows(g), :], last_send.at[g], last_recv.at[g],
            {"angle": other},
        )

    def one(role, carry):
        chunk(role).wait()

        @pl.when(role + AHEAD < count)
        def _():
            chunk(role + AHEAD).start()

        following = jnp.minimum(role + 1, count - 1)
        grow(role + 1, owner(following), factor_ref, spread_ref, grown_ref)
        partial_moments(role, buf, grown_ref, weight_ref, part)

        @pl.when(role == 0)
        def _():
            pl.semaphore_wait(barrier, partners)

        @pl.when(role < 3)
        def _():
            for g in ORDER:
                early_copy(role, g).start()

        @pl.when(role == 5)
        def _():
            for g in ORDER:
                early_copy(0, g).wait_recv()
                part[3, :, 8 * g : 8 * g + 8] += early[0, :, 8 * g : 8 * g + 8]
                half_copy(0, g).start()
                half_copy(1, g).start()

        return carry

    lax.fori_loop(0, count, one, 0)

    for g in ORDER:
        here = slice(8 * g, 8 * g + 8)
        early_copy(1, g).wait_recv()
        early_copy(2, g).wait_recv()
        part[6, :, here] += early[1, :, here] + early[2, :, here]
        last_copy(g).start()
    for g in ORDER:
        here = slice(8 * g, 8 * g + 8)
        half_copy(0, g).wait_recv()
        part[4, 0:3, here] += halves[0, :, here]
        late_copy(0, g).start()
        half_copy(1, g).wait_recv()
        part[5, 3:6, here] += halves[1, :, here]
        late_copy(1, g).start()

    @pl.when(jnp.logical_not(has_last_tile))
    def _():
        up_halo[...] = jnp.zeros_like(up_halo)

    @pl.when(jnp.logical_not(has_next_tile))
    def _():
        down_halo[...] = jnp.zeros_like(down_halo)

    @pl.when(jnp.logical_not(has_last_angle))
    def _():
        left_halo[...] = jnp.zeros_like(left_halo)

    @pl.when(jnp.logical_not(has_next_angle))
    def _():
        right_halo[...] = jnp.zeros_like(right_halo)

    def to_layer(g):
        return remote(
            orient.at[:, rows(g), :], layer_halo.at[:, rows(g), :],
            halo_send.at[0, g], halo_recv.at[0, g], {"layer": 1 - layer},
        )

    def to_next_angle(g):
        return remote(
            orient.at[:, rows(g), LANES:cols], left_halo.at[:, rows(g), :],
            halo_send.at[1, g], halo_recv.at[1, g], {"angle": me + 1},
        )

    def to_last_angle(g):
        return remote(
            orient.at[:, rows(g), 0:LANES], right_halo.at[:, rows(g), :],
            halo_send.at[2, g], halo_recv.at[2, g], {"angle": me - 1},
        )

    to_next_tile = remote(
        orient.at[:, rows(2), :], up_halo, halo_send.at[3, 0], halo_recv.at[3, 0],
        {"tile": tile + 1},
    )
    to_last_tile = remote(
        orient.at[:, rows(0), :], down_halo, halo_send.at[3, 1], halo_recv.at[3, 1],
        {"tile": tile - 1},
    )

    mask_copy.wait()
    for g in ORDER:
        here = slice(8 * g, 8 * g + 8)
        late_copy(0, g).wait_recv()
        late_copy(1, g).wait_recv()
        last_copy(g).wait_recv()
        total = part[7, :, here] + (late[0, :, here] + late[1, :, here]) + last[:, here]
        field = [total[1] / total[0], total[2] / total[0]]
        orient[0, here] = field[0]
        orient[1, here] = field[1]
        to_layer(g).start()
        pl.when(has_next_angle)(lambda: to_next_angle(g).start())
        pl.when(has_last_angle)(lambda: to_last_angle(g).start())
        if g == 0:
            pl.when(has_last_tile)(lambda: to_last_tile.start())
        if g == 2:
            pl.when(has_next_tile)(lambda: to_next_tile.start())
        mask = mask_ref[here].astype(jnp.float32)
        out[0, here] = field[0] * mask
        out[1, here] = field[1] * mask
        out[2, here] = (total[3] / total[0] - field[0] * field[0]) * mask
        out[3, here] = (total[4] / total[0] - field[1] * field[1]) * mask
        out[4, here] = (total[5] / total[0] - field[0] * field[1]) * mask

    pl.when(has_last_tile)(lambda: to_next_tile.wait_recv())
    pl.when(has_next_tile)(lambda: to_last_tile.wait_recv())
    for g in ORDER:
        pl.when(has_last_angle)(lambda: to_next_angle(g).wait_recv())
        pl.when(has_next_angle)(lambda: to_last_angle(g).wait_recv())

    mask = mask_ref[...].astype(jnp.float32)
    lane = lax.broadcasted_iota(jnp.int32, (ROWS, cols), 1)
    row = lax.broadcasted_iota(jnp.int32, (ROWS, cols), 0)
    along_x, along_y = [], []
    for f in range(2):
        field = orient[f]
        after = jnp.where(
            lane == cols - 1, right_halo[f, :, 0:1], pltpu.roll(field, cols - 1, 1)
        )
        before = jnp.where(lane == 0, left_halo[f, :, LANES - 1 : LANES], pltpu.roll(field, 1, 1))
        along_x.append(0.5 * (after - before))
        after = jnp.where(row == ROWS - 1, down_halo[f, 0:1, :], pltpu.roll(field, ROWS - 1, 0))
        before = jnp.where(row == 0, up_halo[f, 7:8, :], pltpu.roll(field, 1, 0))
        along_y.append(0.5 * (after - before))
    out[5] = -along_y[1] * mask
    out[6] = -along_x[0] * mask
    out[7] = -(along_x[0] + along_y[1]) * mask
    out[8] = along_x[1] * mask
    out[9] = along_y[0] * mask
    for g in ORDER:
        to_layer(g).wait_recv()
    slope = (0.5 / LAYER_PITCH) * (1 - 2 * layer).astype(jnp.float32) * mask
    out[10] = layer_halo[0] * slope
    out[11] = layer_halo[1] * slope

    for g in ORDER:
        for role in range(3):
            early_copy(role, g).wait_send()
        for side in range(2):
            half_copy(side, g).wait_send()
            late_copy(side, g).wait_send()
        last_copy(g).wait_send()
        to_layer(g).wait_send()
        pl.when(has_next_angle)(lambda: to_next_angle(g).wait_send())
        pl.when(has_last_angle)(lambda: to_last_angle(g).wait_send())
    pl.when(has_next_tile)(lambda: to_next_tile.wait_send())
    pl.when(has_last_tile)(lambda: to_last_tile.wait_send())


def write_out(maps, orient_out, spread_out, nye_out, sem):
    copies = [
        pltpu.make_async_copy(maps.at[0:2], orient_out, sem.at[0]),
        pltpu.make_async_copy(maps.at[2:5], spread_out, sem.at[1]),
        pltpu.make_async_copy(maps.at[5:12], nye_out, sem.at[2]),
    ]
    for copy in copies:
        copy.start()
    for copy in copies:
        copy.wait()


def on_device(count, tiles, frames, exponents, valid_mask):
    columns = frames.shape[3]
    cols = columns // count
    stack = frames.reshape(HALF, 2 * ROWS, columns)
    codes = exponents[0].transpose(1, 2, 0).reshape(ROWS * 16, ANGLES_HERE)
    f32 = jnp.float32
    bf16 = jnp.bfloat16
    dma = pltpu.SemaphoreType.DMA
    hbm = pl.BlockSpec(memory_space=pltpu.HBM)
    vmem = pl.BlockSpec(memory_space=pltpu.VMEM)
    block = (MOMENTS, ROWS, cols)
    maps = pl.pallas_call(
        functools.partial(kernel, (count, tiles)),
        out_shape=jax.ShapeDtypeStruct((12, ROWS, cols), f32),
        in_specs=[pl.BlockSpec(memory_space=pl.ANY)] * 3,
        out_specs=vmem,
        scratch_shapes=[
            pltpu.VMEM((count, HALF, 2 * ROWS, cols), bf16),
            pltpu.VMEM((ROWS * 16, ANGLES_HERE), jnp.int32),
            pltpu.VMEM((ROWS, cols), jnp.int32),
            pltpu.VMEM((16, 48, 2 * ANGLES_HERE), bf16),
            pltpu.VMEM((2 * ANGLES_HERE, DEPTH), bf16),
            pltpu.VMEM((3, MOMENTS, 16, DEPTH), bf16),
            pltpu.VMEM((2, 96, DEPTH), bf16),
            pltpu.VMEM((count,) + block, f32),
            pltpu.VMEM((3,) + block, f32),
            pltpu.VMEM((2, 3, ROWS, cols), f32),
            pltpu.VMEM((2,) + block, f32),
            pltpu.VMEM(block, f32),
            pltpu.VMEM((2, ROWS, cols), f32),
            pltpu.VMEM((2, ROWS, LANES), f32),
            pltpu.VMEM((2, ROWS, LANES), f32),
            pltpu.VMEM((2, 8, cols), f32),
            pltpu.VMEM((2, 8, cols), f32),
            pltpu.VMEM((2, ROWS, cols), f32),
            dma((count,)), dma((2,)), dma((3, 3)), dma((3, 3)), dma((2, 3)), dma((2, 3)),
            dma((2, 3)), dma((2, 3)), dma((3,)), dma((3,)), dma((4, 3)), dma((4, 3)),
        ],
        compiler_params=pltpu.CompilerParams(
            collective_id=0, has_side_effects=True, vmem_limit_bytes=52 * 1024 * 1024
        ),
    )(*(pltpu.with_memory_space_constraint(a, pltpu.HBM) for a in (stack, codes, valid_mask[0])))
    out = pl.pallas_call(
        write_out,
        out_shape=[jax.ShapeDtypeStruct((n, ROWS, cols), f32) for n in (2, 3, 7)],
        in_specs=[pl.BlockSpec(memory_space=pl.ANY)],
        out_specs=[hbm] * 3,
        scratch_shapes=[dma((3,))],
        compiler_params=pltpu.CompilerParams(vmem_limit_bytes=1024 * 1024),
    )(maps)
    return tuple(one[:, None] for one in out)


def solution(mesh):
    in_specs = (
        P("layer", "angle", "tile", None),
        P("layer", "angle", "tile", None),
        P("layer", "tile", "angle"),
    )
    out_specs = (
        P(None, "layer", "tile", "angle"),
        P(None, "layer", "tile", "angle"),
        P(None, "layer", "tile", "angle"),
    )
    return jax.shard_map(
        functools.partial(on_device, mesh.shape["angle"], mesh.shape["tile"]),
        mesh=mesh, in_specs=in_specs, out_specs=out_specs, check_vma=False,
    )
```

```python
import functools

import jax
import jax.numpy as jnp
from jax import lax
from jax.experimental import pallas as pl
from jax.experimental.pallas import tpu as pltpu
from jax.sharding import PartitionSpec as P

NPHI = 32
NCHI = 32
MOMENTS = 6
ROWS = 24
ANGLES_HERE = 128
LANES = 128
HALF = ANGLES_HERE // 2
DEPTH = HALF * 16
LAYER_PITCH = 2.0
AHEAD = 3
ORDER = (0, 2, 1)
MESH = pl.DeviceIdType.MESH


def fill_tables(me, spread_ref, weight_ref):
    lane = lax.broadcasted_iota(jnp.int32, (ANGLES_HERE, DEPTH), 1)
    source = lax.broadcasted_iota(jnp.int32, (ANGLES_HERE, DEPTH), 0)
    pair = lane >> 4
    for parity in range(2):
        hit = source == 2 * pair + parity
        spread_ref[parity * ANGLES_HERE : (parity + 1) * ANGLES_HERE, :] = jnp.where(
            hit, 1.0, 0.0
        ).astype(jnp.bfloat16)
    lane = lax.broadcasted_iota(jnp.int32, (16, DEPTH), 1)
    row = lax.broadcasted_iota(jnp.int32, (16, DEPTH), 0)
    inner = lane & 15
    keep = inner == row
    for kind in range(3):
        if kind == 0:
            parity = 0
        elif kind == 2:
            parity = 1
        else:
            parity = inner >> 3
        angle = me * ANGLES_HERE + 2 * (lane >> 4) + parity
        phi = ((angle >> 5).astype(jnp.float32) - 0.5 * (NPHI - 1)) / (0.5 * NPHI)
        chi = ((angle & 31).astype(jnp.float32) - 0.5 * (NCHI - 1)) / (0.5 * NCHI)
        rows = (jnp.ones_like(phi), phi, chi, phi * phi, chi * chi, phi * chi)
        for m in range(MOMENTS):
            weight_ref[kind, m] = jnp.where(keep, rows[m], 0.0).astype(jnp.bfloat16)


def fill_factors(exp_ref, factor_ref):
    blank = jnp.zeros((8, ANGLES_HERE), jnp.float32)

    def one(k, carry):
        code = exp_ref[pl.ds(k, ROWS, stride=16), :]
        factor = jnp.exp2(code.astype(jnp.float32))
        low, mid, high = factor[0:8], factor[8:16], factor[16:24]
        even = jnp.concatenate([low, mid, high, blank, blank, blank], axis=0)
        odd = jnp.concatenate([blank, blank, blank, low, mid, high], axis=0)
        both = jnp.concatenate([even, odd], axis=1)
        factor_ref[k] = both.astype(jnp.bfloat16)
        return carry

    lax.fori_loop(0, 16, one, 0)


def grow(role, dest, factor_ref, spread_ref, grown_ref):
    both = factor_ref[pl.ds(2 * dest, 2)].reshape(96, 2 * ANGLES_HERE)
    grown_ref[lax.rem(role, 2)] = jnp.dot(
        both, spread_ref[...], preferred_element_type=jnp.float32
    ).astype(jnp.bfloat16)


def partial_moments(role, buf, grown_ref, weight_ref, part):
    slot = lax.rem(role, 2)
    for side in range(2):
        sums = []
        for kind in range(3):
            begin = side * 48 + kind * 16
            left = (weight_ref[kind] * grown_ref[slot, begin : begin + 16][None]).reshape(
                MOMENTS * 16, DEPTH
            )
            right = buf[
                role, :, kind * 16 : kind * 16 + 16, side * LANES : (side + 1) * LANES
            ].reshape(DEPTH, LANES)
            sums.append(
                jnp.dot(left, right, preferred_element_type=jnp.float32).reshape(
                    MOMENTS, 16, LANES
                )
            )
        first, second, third = sums
        here = slice(side * LANES, (side + 1) * LANES)
        part[role, :, 0:8, here] = first[:, 0:8] + second[:, 8:16]
        part[role, :, 8:16, here] = first[:, 8:16] + third[:, 0:8]
        part[role, :, 16:24, here] = second[:, 0:8] + third[:, 8:16]


def kernel(
    sizes, frames, exponents, valid, out,
    buf, exp_ref, mask_ref, factor_ref, spread_ref, weight_ref, grown_ref,
    part, early, far, late, last, orient,
    left_halo, right_halo, up_halo, down_halo, layer_halo,
    in_sem, small_sem, early_send, early_recv, far_send, far_recv,
    late_send, late_recv, last_send, last_recv, halo_send, halo_recv,
):
    count, tiles = sizes
    ring = count // 2
    me = lax.axis_index("angle")
    tile = lax.axis_index("tile")
    layer = lax.axis_index("layer")
    cols = 2 * LANES
    px, py = me // ring, lax.rem(me, ring)
    other = (1 - px) * ring + py
    above = px * ring + lax.rem(py + 1, ring)
    below = px * ring + lax.rem(py + ring - 1, ring)
    across = px * ring + lax.rem(py + 2, ring)
    has_next_tile = tile < tiles - 1
    has_last_tile = tile > 0
    has_next_angle = me < count - 1
    has_last_angle = me > 0
    far_next = me == ring - 1
    far_last = me == ring

    def owner(role):
        swap = jnp.logical_or(role < 3, role == 6)
        turn = lax.rem(role, 3)
        shift = jnp.where(role < 6, jnp.where(turn == 0, 2, jnp.where(turn == 1, 1, ring - 1)), 0)
        return jnp.where(swap, 1 - px, px) * ring + lax.rem(py + shift, ring)

    def chunk(role):
        begin = pl.multiple_of(owner(role) * cols, cols)
        return pltpu.make_async_copy(
            frames.at[:, :, pl.ds(begin, cols)], buf.at[role], in_sem.at[role]
        )

    exp_copy = pltpu.make_async_copy(exponents, exp_ref, small_sem.at[0])
    mask_copy = pltpu.make_async_copy(valid, mask_ref, small_sem.at[1])
    exp_copy.start()
    for role in range(AHEAD):
        chunk(jnp.int32(role)).start()

    barrier = pltpu.get_barrier_semaphore()

    def greet(where):
        pl.semaphore_signal(barrier, inc=1, device_id=where, device_id_type=MESH)

    greet({"angle": other})
    greet({"angle": above})
    greet({"angle": below})
    greet({"angle": across})
    greet({"layer": 1 - layer})
    pl.when(has_last_tile)(lambda: greet({"tile": tile - 1}))
    pl.when(has_next_tile)(lambda: greet({"tile": tile + 1}))
    pl.when(far_next)(lambda: greet({"angle": me + 1}))
    pl.when(far_last)(lambda: greet({"angle": me - 1}))
    partners = 5
    for present in (has_last_tile, has_next_tile, far_next, far_last):
        partners = partners + present.astype(jnp.int32)

    fill_tables(me, spread_ref, weight_ref)
    exp_copy.wait()
    mask_copy.start()
    fill_factors(exp_ref, factor_ref)
    grow(jnp.int32(0), owner(jnp.int32(0)), factor_ref, spread_ref, grown_ref)

    def remote(src, dst, send, recv, where):
        return pltpu.make_async_remote_copy(
            src_ref=src, dst_ref=dst, send_sem=send, recv_sem=recv, device_id=where,
            device_id_type=MESH,
        )

    def rows(g):
        return pl.ds(8 * g, 8)

    def early_copy(role, g):
        to = jnp.where(role == 0, other, jnp.where(role == 1, above, below))
        return remote(
            part.at[role, :, rows(g), :], early.at[role, :, rows(g), :],
            early_send.at[role, g], early_recv.at[role, g], {"angle": to},
        )

    def far_copy(g):
        return remote(
            part.at[3, :, rows(g), :], far.at[:, rows(g), :], far_send.at[g], far_recv.at[g],
            {"angle": across},
        )

    def late_copy(side):
        return remote(
            part.at[4 + side], late.at[side], late_send.at[side], late_recv.at[side],
            {"angle": below if side else above},
        )

    def last_copy(g):
        return remote(
            part.at[6, :, rows(g), :], last.at[:, rows(g), :], last_send.at[g], last_recv.at[g],
            {"angle": other},
        )

    def one(role, carry):
        chunk(role).wait()

        @pl.when(role + AHEAD < count)
        def _():
            chunk(role + AHEAD).start()

        following = jnp.minimum(role + 1, count - 1)
        grow(role + 1, owner(following), factor_ref, spread_ref, grown_ref)
        partial_moments(role, buf, grown_ref, weight_ref, part)

        @pl.when(role == 0)
        def _():
            pl.semaphore_wait(barrier, partners)

        @pl.when(role < 3)
        def _():
            for g in ORDER:
                early_copy(role, g).start()

        for side in range(2):

            @pl.when(role == 4 + side)
            def _():
                late_copy(side).start()

        return carry

    lax.fori_loop(0, count, one, 0)

    for g in ORDER:
        early_copy(0, g).wait_recv()
        part[3, :, 8 * g : 8 * g + 8] += early[0, :, 8 * g : 8 * g + 8]
        far_copy(g).start()
    for g in ORDER:
        here = slice(8 * g, 8 * g + 8)
        early_copy(1, g).wait_recv()
        early_copy(2, g).wait_recv()
        part[6, :, here] += early[1, :, here] + early[2, :, here]
        last_copy(g).start()
    @pl.when(jnp.logical_not(has_last_tile))
    def _():
        up_halo[...] = jnp.zeros_like(up_halo)

    @pl.when(jnp.logical_not(has_next_tile))
    def _():
        down_halo[...] = jnp.zeros_like(down_halo)

    @pl.when(jnp.logical_not(has_last_angle))
    def _():
        left_halo[...] = jnp.zeros_like(left_halo)

    @pl.when(jnp.logical_not(has_next_angle))
    def _():
        right_halo[...] = jnp.zeros_like(right_halo)

    def to_layer(g):
        return remote(
            orient.at[:, rows(g), :], layer_halo.at[:, rows(g), :],
            halo_send.at[0, g], halo_recv.at[0, g], {"layer": 1 - layer},
        )

    def to_next_angle(g):
        return remote(
            orient.at[:, rows(g), LANES:cols], left_halo.at[:, rows(g), :],
            halo_send.at[1, g], halo_recv.at[1, g], {"angle": me + 1},
        )

    def to_last_angle(g):
        return remote(
            orient.at[:, rows(g), 0:LANES], right_halo.at[:, rows(g), :],
            halo_send.at[2, g], halo_recv.at[2, g], {"angle": me - 1},
        )

    to_next_tile = remote(
        orient.at[:, rows(2), :], up_halo, halo_send.at[3, 0], halo_recv.at[3, 0],
        {"tile": tile + 1},
    )
    to_last_tile = remote(
        orient.at[:, rows(0), :], down_halo, halo_send.at[3, 1], halo_recv.at[3, 1],
        {"tile": tile - 1},
    )

    mask_copy.wait()
    for side in range(2):
        late_copy(side).wait_recv()
    for g in ORDER:
        here = slice(8 * g, 8 * g + 8)
        far_copy(g).wait_recv()
        last_copy(g).wait_recv()
        total = (part[7, :, here] + far[:, here]) + (late[0, :, here] + late[1, :, here])
        total = total + last[:, here]
        field = [total[1] / total[0], total[2] / total[0]]
        orient[0, here] = field[0]
        orient[1, here] = field[1]
        to_layer(g).start()
        pl.when(has_next_angle)(lambda: to_next_angle(g).start())
        pl.when(has_last_angle)(lambda: to_last_angle(g).start())
        if g == 0:
            pl.when(has_last_tile)(lambda: to_last_tile.start())
        if g == 2:
            pl.when(has_next_tile)(lambda: to_next_tile.start())
        mask = mask_ref[here].astype(jnp.float32)
        out[0, here] = field[0] * mask
        out[1, here] = field[1] * mask
        out[2, here] = (total[3] / total[0] - field[0] * field[0]) * mask
        out[3, here] = (total[4] / total[0] - field[1] * field[1]) * mask
        out[4, here] = (total[5] / total[0] - field[0] * field[1]) * mask

    pl.when(has_last_tile)(lambda: to_next_tile.wait_recv())
    pl.when(has_next_tile)(lambda: to_last_tile.wait_recv())
    for g in ORDER:
        pl.when(has_last_angle)(lambda: to_next_angle(g).wait_recv())
        pl.when(has_next_angle)(lambda: to_last_angle(g).wait_recv())

    mask = mask_ref[...].astype(jnp.float32)
    lane = lax.broadcasted_iota(jnp.int32, (ROWS, cols), 1)
    row = lax.broadcasted_iota(jnp.int32, (ROWS, cols), 0)
    along_x, along_y = [], []
    for f in range(2):
        field = orient[f]
        after = jnp.where(
            lane == cols - 1, right_halo[f, :, 0:1], pltpu.roll(field, cols - 1, 1)
        )
        before = jnp.where(lane == 0, left_halo[f, :, LANES - 1 : LANES], pltpu.roll(field, 1, 1))
        along_x.append(0.5 * (after - before))
        after = jnp.where(row == ROWS - 1, down_halo[f, 0:1, :], pltpu.roll(field, ROWS - 1, 0))
        before = jnp.where(row == 0, up_halo[f, 7:8, :], pltpu.roll(field, 1, 0))
        along_y.append(0.5 * (after - before))
    out[5] = -along_y[1] * mask
    out[6] = -along_x[0] * mask
    out[7] = -(along_x[0] + along_y[1]) * mask
    out[8] = along_x[1] * mask
    out[9] = along_y[0] * mask
    for g in ORDER:
        to_layer(g).wait_recv()
    slope = (0.5 / LAYER_PITCH) * (1 - 2 * layer).astype(jnp.float32) * mask
    out[10] = layer_halo[0] * slope
    out[11] = layer_halo[1] * slope

    for g in ORDER:
        for role in range(3):
            early_copy(role, g).wait_send()
        far_copy(g).wait_send()
        last_copy(g).wait_send()
        to_layer(g).wait_send()
        pl.when(has_next_angle)(lambda: to_next_angle(g).wait_send())
        pl.when(has_last_angle)(lambda: to_last_angle(g).wait_send())
    for side in range(2):
        late_copy(side).wait_send()
    pl.when(has_next_tile)(lambda: to_next_tile.wait_send())
    pl.when(has_last_tile)(lambda: to_last_tile.wait_send())


def write_out(maps, orient_out, spread_out, nye_out, sem):
    copies = [
        pltpu.make_async_copy(maps.at[0:2], orient_out, sem.at[0]),
        pltpu.make_async_copy(maps.at[2:5], spread_out, sem.at[1]),
        pltpu.make_async_copy(maps.at[5:12], nye_out, sem.at[2]),
    ]
    for copy in copies:
        copy.start()
    for copy in copies:
        copy.wait()


def on_device(count, tiles, frames, exponents, valid_mask):
    columns = frames.shape[3]
    cols = columns // count
    stack = frames.reshape(HALF, 2 * ROWS, columns)
    codes = exponents[0].transpose(1, 2, 0).reshape(ROWS * 16, ANGLES_HERE)
    f32 = jnp.float32
    bf16 = jnp.bfloat16
    dma = pltpu.SemaphoreType.DMA
    hbm = pl.BlockSpec(memory_space=pltpu.HBM)
    vmem = pl.BlockSpec(memory_space=pltpu.VMEM)
    block = (MOMENTS, ROWS, cols)
    maps = pl.pallas_call(
        functools.partial(kernel, (count, tiles)),
        out_shape=jax.ShapeDtypeStruct((12, ROWS, cols), f32),
        in_specs=[pl.BlockSpec(memory_space=pl.ANY)] * 3,
        out_specs=vmem,
        scratch_shapes=[
            pltpu.VMEM((count, HALF, 2 * ROWS, cols), bf16),
            pltpu.VMEM((ROWS * 16, ANGLES_HERE), jnp.int32),
            pltpu.VMEM((ROWS, cols), jnp.int32),
            pltpu.VMEM((16, 48, 2 * ANGLES_HERE), bf16),
            pltpu.VMEM((2 * ANGLES_HERE, DEPTH), bf16),
            pltpu.VMEM((3, MOMENTS, 16, DEPTH), bf16),
            pltpu.VMEM((2, 96, DEPTH), bf16),
            pltpu.VMEM((count,) + block, f32),
            pltpu.VMEM((3,) + block, f32),
            pltpu.VMEM(block, f32),
            pltpu.VMEM((2,) + block, f32),
            pltpu.VMEM(block, f32),
            pltpu.VMEM((2, ROWS, cols), f32),
            pltpu.VMEM((2, ROWS, LANES), f32),
            pltpu.VMEM((2, ROWS, LANES), f32),
            pltpu.VMEM((2, 8, cols), f32),
            pltpu.VMEM((2, 8, cols), f32),
            pltpu.VMEM((2, ROWS, cols), f32),
            dma((count,)), dma((2,)), dma((3, 3)), dma((3, 3)), dma((3,)), dma((3,)),
            dma((2,)), dma((2,)), dma((3,)), dma((3,)), dma((4, 3)), dma((4, 3)),
        ],
        compiler_params=pltpu.CompilerParams(
            collective_id=0, has_side_effects=True, vmem_limit_bytes=52 * 1024 * 1024
        ),
    )(*(pltpu.with_memory_space_constraint(a, pltpu.HBM) for a in (stack, codes, valid_mask[0])))
    out = pl.pallas_call(
        write_out,
        out_shape=[jax.ShapeDtypeStruct((n, ROWS, cols), f32) for n in (2, 3, 7)],
        in_specs=[pl.BlockSpec(memory_space=pl.ANY)],
        out_specs=[hbm] * 3,
        scratch_shapes=[dma((3,))],
        compiler_params=pltpu.CompilerParams(vmem_limit_bytes=1024 * 1024),
    )(maps)
    return tuple(one[:, None] for one in out)


def solution(mesh):
    in_specs = (
        P("layer", "angle", "tile", None),
        P("layer", "angle", "tile", None),
        P("layer", "tile", "angle"),
    )
    out_specs = (
        P(None, "layer", "tile", "angle"),
        P(None, "layer", "tile", "angle"),
        P(None, "layer", "tile", "angle"),
    )
    return jax.shard_map(
        functools.partial(on_device, mesh.shape["angle"], mesh.shape["tile"]),
        mesh=mesh, in_specs=in_specs, out_specs=out_specs, check_vma=False,
    )
```

```python
import functools

import jax
import jax.numpy as jnp
from jax import lax
from jax.experimental import pallas as pl
from jax.experimental.pallas import tpu as pltpu
from jax.sharding import PartitionSpec as P

NPHI = 32
NCHI = 32
MOMENTS = 6
ROWS = 24
ANGLES_HERE = 128
LANES = 128
HALF = ANGLES_HERE // 2
DEPTH = HALF * 16
LAYER_PITCH = 2.0
AHEAD = 3
ORDER = (0, 2, 1)
MESH = pl.DeviceIdType.MESH


def fill_tables(me, spread_ref, weight_ref):
    lane = lax.broadcasted_iota(jnp.int32, (ANGLES_HERE, DEPTH), 1)
    source = lax.broadcasted_iota(jnp.int32, (ANGLES_HERE, DEPTH), 0)
    pair = lane >> 4
    for parity in range(2):
        hit = source == 2 * pair + parity
        spread_ref[parity * ANGLES_HERE : (parity + 1) * ANGLES_HERE, :] = jnp.where(
            hit, 1.0, 0.0
        ).astype(jnp.bfloat16)
    lane = lax.broadcasted_iota(jnp.int32, (16, DEPTH), 1)
    row = lax.broadcasted_iota(jnp.int32, (16, DEPTH), 0)
    inner = lane & 15
    keep = inner == row
    for kind in range(3):
        if kind == 0:
            parity = 0
        elif kind == 2:
            parity = 1
        else:
            parity = inner >> 3
        angle = me * ANGLES_HERE + 2 * (lane >> 4) + parity
        phi = ((angle >> 5).astype(jnp.float32) - 0.5 * (NPHI - 1)) / (0.5 * NPHI)
        chi = ((angle & 31).astype(jnp.float32) - 0.5 * (NCHI - 1)) / (0.5 * NCHI)
        rows = (jnp.ones_like(phi), phi, chi, phi * phi, chi * chi, phi * chi)
        for m in range(MOMENTS):
            weight_ref[kind, m] = jnp.where(keep, rows[m], 0.0).astype(jnp.bfloat16)


def fill_factors(exp_ref, factor_ref):
    blank = jnp.zeros((8, ANGLES_HERE), jnp.float32)

    def one(k, carry):
        code = exp_ref[pl.ds(k, ROWS, stride=16), :]
        factor = jnp.exp2(code.astype(jnp.float32))
        low, mid, high = factor[0:8], factor[8:16], factor[16:24]
        even = jnp.concatenate([low, mid, high, blank, blank, blank], axis=0)
        odd = jnp.concatenate([blank, blank, blank, low, mid, high], axis=0)
        both = jnp.concatenate([even, odd], axis=1)
        factor_ref[k] = both.astype(jnp.bfloat16)
        return carry

    lax.fori_loop(0, 16, one, 0)


def grow(step, dest, factor_ref, spread_ref, grown_ref):
    both = factor_ref[pl.ds(2 * dest, 2)].reshape(96, 2 * ANGLES_HERE)
    grown_ref[lax.rem(step, 2)] = jnp.dot(
        both, spread_ref[...], preferred_element_type=jnp.float32
    ).astype(jnp.bfloat16)


def partial_moments(step, role, buf, grown_ref, weight_ref, part):
    slot = lax.rem(step, 2)
    for side in range(2):
        sums = []
        for kind in range(3):
            begin = side * 48 + kind * 16
            left = (weight_ref[kind] * grown_ref[slot, begin : begin + 16][None]).reshape(
                MOMENTS * 16, DEPTH
            )
            right = buf[
                role, :, kind * 16 : kind * 16 + 16, side * LANES : (side + 1) * LANES
            ].reshape(DEPTH, LANES)
            sums.append(
                jnp.dot(left, right, preferred_element_type=jnp.float32).reshape(
                    MOMENTS, 16, LANES
                )
            )
        first, second, third = sums
        here = slice(side * LANES, (side + 1) * LANES)
        part[role, :, 0:8, here] = first[:, 0:8] + second[:, 8:16]
        part[role, :, 8:16, here] = first[:, 8:16] + third[:, 0:8]
        part[role, :, 16:24, here] = second[:, 0:8] + third[:, 8:16]


def kernel(
    sizes, frames, exponents, valid, out,
    buf, exp_ref, mask_ref, factor_ref, spread_ref, weight_ref, grown_ref,
    part, early, far, late, last, orient,
    left_halo, right_halo, up_halo, down_halo, layer_halo,
    in_sem, small_sem, early_send, early_recv, far_send, far_recv,
    late_send, late_recv, last_send, last_recv, halo_send, halo_recv,
):
    count, tiles = sizes
    ring = count // 2
    me = lax.axis_index("angle")
    tile = lax.axis_index("tile")
    layer = lax.axis_index("layer")
    cols = 2 * LANES
    px, py = me // ring, lax.rem(me, ring)
    other = (1 - px) * ring + py
    above = px * ring + lax.rem(py + 1, ring)
    below = px * ring + lax.rem(py + ring - 1, ring)
    across = px * ring + lax.rem(py + 2, ring)
    has_next_tile = tile < tiles - 1
    has_last_tile = tile > 0
    has_next_angle = me < count - 1
    has_last_angle = me > 0
    far_next = me == ring - 1
    far_last = me == ring

    def owner(role):
        swap = jnp.logical_or(role < 3, role == 6)
        turn = lax.rem(role, 3)
        shift = jnp.where(role < 6, jnp.where(turn == 0, 2, jnp.where(turn == 1, 1, ring - 1)), 0)
        return jnp.where(swap, 1 - px, px) * ring + lax.rem(py + shift, ring)

    def role_at(step):
        return jnp.where(step < 2, 1 - step, step)

    def chunk(role):
        begin = pl.multiple_of(owner(role) * cols, cols)
        return pltpu.make_async_copy(
            frames.at[:, :, pl.ds(begin, cols)], buf.at[role], in_sem.at[role]
        )

    exp_copy = pltpu.make_async_copy(exponents, exp_ref, small_sem.at[0])
    mask_copy = pltpu.make_async_copy(valid, mask_ref, small_sem.at[1])
    exp_copy.start()
    for role in range(AHEAD):
        chunk(role_at(jnp.int32(role))).start()

    barrier = pltpu.get_barrier_semaphore()

    def greet(where):
        pl.semaphore_signal(barrier, inc=1, device_id=where, device_id_type=MESH)

    greet({"angle": other})
    greet({"angle": above})
    greet({"angle": below})
    greet({"angle": across})
    greet({"layer": 1 - layer})
    pl.when(has_last_tile)(lambda: greet({"tile": tile - 1}))
    pl.when(has_next_tile)(lambda: greet({"tile": tile + 1}))
    pl.when(far_next)(lambda: greet({"angle": me + 1}))
    pl.when(far_last)(lambda: greet({"angle": me - 1}))
    partners = 5
    for present in (has_last_tile, has_next_tile, far_next, far_last):
        partners = partners + present.astype(jnp.int32)

    fill_tables(me, spread_ref, weight_ref)
    exp_copy.wait()
    mask_copy.start()
    fill_factors(exp_ref, factor_ref)
    grow(jnp.int32(0), owner(role_at(jnp.int32(0))), factor_ref, spread_ref, grown_ref)

    def remote(src, dst, send, recv, where):
        return pltpu.make_async_remote_copy(
            src_ref=src, dst_ref=dst, send_sem=send, recv_sem=recv, device_id=where,
            device_id_type=MESH,
        )

    def rows(g):
        return pl.ds(8 * g, 8)

    def early_copy(role, g):
        to = jnp.where(role == 0, other, jnp.where(role == 1, above, below))
        return remote(
            part.at[role, :, rows(g), :], early.at[role, :, rows(g), :],
            early_send.at[role, g], early_recv.at[role, g], {"angle": to},
        )

    def far_copy(g):
        return remote(
            part.at[3, :, rows(g), :], far.at[:, rows(g), :], far_send.at[g], far_recv.at[g],
            {"angle": across},
        )

    def late_copy(side):
        return remote(
            part.at[4 + side], late.at[side], late_send.at[side], late_recv.at[side],
            {"angle": below if side else above},
        )

    def last_copy(g):
        return remote(
            part.at[6, :, rows(g), :], last.at[:, rows(g), :], last_send.at[g], last_recv.at[g],
            {"angle": other},
        )

    def one(step, carry):
        role = role_at(step)
        chunk(role).wait()

        @pl.when(step + AHEAD < count)
        def _():
            chunk(step + AHEAD).start()

        following = jnp.minimum(step + 1, count - 1)
        grow(step + 1, owner(role_at(following)), factor_ref, spread_ref, grown_ref)
        partial_moments(step, role, buf, grown_ref, weight_ref, part)

        @pl.when(step == 0)
        def _():
            pl.semaphore_wait(barrier, partners)

        @pl.when(role < 3)
        def _():
            for g in ORDER:
                early_copy(role, g).start()

        for side in range(2):

            @pl.when(role == 4 + side)
            def _():
                late_copy(side).start()

        return carry

    lax.fori_loop(0, count, one, 0)

    for g in ORDER:
        early_copy(0, g).wait_recv()
        part[3, :, 8 * g : 8 * g + 8] += early[0, :, 8 * g : 8 * g + 8]
        far_copy(g).start()
    for g in ORDER:
        here = slice(8 * g, 8 * g + 8)
        early_copy(1, g).wait_recv()
        early_copy(2, g).wait_recv()
        part[6, :, here] += early[1, :, here] + early[2, :, here]
        last_copy(g).start()
    @pl.when(jnp.logical_not(has_last_tile))
    def _():
        up_halo[...] = jnp.zeros_like(up_halo)

    @pl.when(jnp.logical_not(has_next_tile))
    def _():
        down_halo[...] = jnp.zeros_like(down_halo)

    @pl.when(jnp.logical_not(has_last_angle))
    def _():
        left_halo[...] = jnp.zeros_like(left_halo)

    @pl.when(jnp.logical_not(has_next_angle))
    def _():
        right_halo[...] = jnp.zeros_like(right_halo)

    def to_layer(g):
        return remote(
            orient.at[:, rows(g), :], layer_halo.at[:, rows(g), :],
            halo_send.at[0, g], halo_recv.at[0, g], {"layer": 1 - layer},
        )

    def to_next_angle(g):
        return remote(
            orient.at[:, rows(g), LANES:cols], left_halo.at[:, rows(g), :],
            halo_send.at[1, g], halo_recv.at[1, g], {"angle": me + 1},
        )

    def to_last_angle(g):
        return remote(
            orient.at[:, rows(g), 0:LANES], right_halo.at[:, rows(g), :],
            halo_send.at[2, g], halo_recv.at[2, g], {"angle": me - 1},
        )

    to_next_tile = remote(
        orient.at[:, rows(2), :], up_halo, halo_send.at[3, 0], halo_recv.at[3, 0],
        {"tile": tile + 1},
    )
    to_last_tile = remote(
        orient.at[:, rows(0), :], down_halo, halo_send.at[3, 1], halo_recv.at[3, 1],
        {"tile": tile - 1},
    )

    for side in range(2):
        late_copy(side).wait_recv()
    for g in ORDER:
        here = slice(8 * g, 8 * g + 8)
        far_copy(g).wait_recv()
        last_copy(g).wait_recv()
        total = (part[7, :, here] + far[:, here]) + (late[0, :, here] + late[1, :, here])
        total = total + last[:, here]
        field = [total[1] / total[0], total[2] / total[0]]
        orient[0, here] = field[0]
        orient[1, here] = field[1]
        part[7, :, here] = total
        pl.when(has_next_angle)(lambda: to_next_angle(g).start())
        pl.when(has_last_angle)(lambda: to_last_angle(g).start())
        if g == 0:
            pl.when(has_last_tile)(lambda: to_last_tile.start())
        if g == 2:
            pl.when(has_next_tile)(lambda: to_next_tile.start())
        to_layer(g).start()
    mask_copy.wait()
    for g in ORDER:
        here = slice(8 * g, 8 * g + 8)
        mask = mask_ref[here].astype(jnp.float32)
        out[0, here] = orient[0, here] * mask
        out[1, here] = orient[1, here] * mask
        zeroth = part[7, 0, here]
        out[2, here] = (part[7, 3, here] / zeroth - orient[0, here] * orient[0, here]) * mask
        out[3, here] = (part[7, 4, here] / zeroth - orient[1, here] * orient[1, here]) * mask
        out[4, here] = (part[7, 5, here] / zeroth - orient[0, here] * orient[1, here]) * mask

    pl.when(has_last_tile)(lambda: to_next_tile.wait_recv())
    pl.when(has_next_tile)(lambda: to_last_tile.wait_recv())
    for g in ORDER:
        pl.when(has_last_angle)(lambda: to_next_angle(g).wait_recv())
        pl.when(has_next_angle)(lambda: to_last_angle(g).wait_recv())

    mask = mask_ref[...].astype(jnp.float32)
    lane = lax.broadcasted_iota(jnp.int32, (ROWS, cols), 1)
    row = lax.broadcasted_iota(jnp.int32, (ROWS, cols), 0)
    along_x, along_y = [], []
    for f in range(2):
        field = orient[f]
        after = jnp.where(
            lane == cols - 1, right_halo[f, :, 0:1], pltpu.roll(field, cols - 1, 1)
        )
        before = jnp.where(lane == 0, left_halo[f, :, LANES - 1 : LANES], pltpu.roll(field, 1, 1))
        along_x.append(0.5 * (after - before))
        after = jnp.where(row == ROWS - 1, down_halo[f, 0:1, :], pltpu.roll(field, ROWS - 1, 0))
        before = jnp.where(row == 0, up_halo[f, 7:8, :], pltpu.roll(field, 1, 0))
        along_y.append(0.5 * (after - before))
    out[5] = -along_y[1] * mask
    out[6] = -along_x[0] * mask
    out[7] = -(along_x[0] + along_y[1]) * mask
    out[8] = along_x[1] * mask
    out[9] = along_y[0] * mask
    for g in ORDER:
        to_layer(g).wait_recv()
    slope = (0.5 / LAYER_PITCH) * (1 - 2 * layer).astype(jnp.float32) * mask
    out[10] = layer_halo[0] * slope
    out[11] = layer_halo[1] * slope

    for g in ORDER:
        for role in range(3):
            early_copy(role, g).wait_send()
        far_copy(g).wait_send()
        last_copy(g).wait_send()
        to_layer(g).wait_send()
        pl.when(has_next_angle)(lambda: to_next_angle(g).wait_send())
        pl.when(has_last_angle)(lambda: to_last_angle(g).wait_send())
    for side in range(2):
        late_copy(side).wait_send()
    pl.when(has_next_tile)(lambda: to_next_tile.wait_send())
    pl.when(has_last_tile)(lambda: to_last_tile.wait_send())


def write_out(maps, orient_out, spread_out, nye_out, sem):
    copies = [
        pltpu.make_async_copy(maps.at[0:2], orient_out, sem.at[0]),
        pltpu.make_async_copy(maps.at[2:5], spread_out, sem.at[1]),
        pltpu.make_async_copy(maps.at[5:12], nye_out, sem.at[2]),
    ]
    for copy in copies:
        copy.start()
    for copy in copies:
        copy.wait()


def on_device(count, tiles, frames, exponents, valid_mask):
    columns = frames.shape[3]
    cols = columns // count
    stack = frames.reshape(HALF, 2 * ROWS, columns)
    codes = exponents[0].transpose(1, 2, 0).reshape(ROWS * 16, ANGLES_HERE)
    f32 = jnp.float32
    bf16 = jnp.bfloat16
    dma = pltpu.SemaphoreType.DMA
    hbm = pl.BlockSpec(memory_space=pltpu.HBM)
    vmem = pl.BlockSpec(memory_space=pltpu.VMEM)
    block = (MOMENTS, ROWS, cols)
    maps = pl.pallas_call(
        functools.partial(kernel, (count, tiles)),
        out_shape=jax.ShapeDtypeStruct((12, ROWS, cols), f32),
        in_specs=[pl.BlockSpec(memory_space=pl.ANY)] * 3,
        out_specs=vmem,
        scratch_shapes=[
            pltpu.VMEM((count, HALF, 2 * ROWS, cols), bf16),
            pltpu.VMEM((ROWS * 16, ANGLES_HERE), jnp.int32),
            pltpu.VMEM((ROWS, cols), jnp.int32),
            pltpu.VMEM((16, 48, 2 * ANGLES_HERE), bf16),
            pltpu.VMEM((2 * ANGLES_HERE, DEPTH), bf16),
            pltpu.VMEM((3, MOMENTS, 16, DEPTH), bf16),
            pltpu.VMEM((2, 96, DEPTH), bf16),
            pltpu.VMEM((count,) + block, f32),
            pltpu.VMEM((3,) + block, f32),
            pltpu.VMEM(block, f32),
            pltpu.VMEM((2,) + block, f32),
            pltpu.VMEM(block, f32),
            pltpu.VMEM((2, ROWS, cols), f32),
            pltpu.VMEM((2, ROWS, LANES), f32),
            pltpu.VMEM((2, ROWS, LANES), f32),
            pltpu.VMEM((2, 8, cols), f32),
            pltpu.VMEM((2, 8, cols), f32),
            pltpu.VMEM((2, ROWS, cols), f32),
            dma((count,)), dma((2,)), dma((3, 3)), dma((3, 3)), dma((3,)), dma((3,)),
            dma((2,)), dma((2,)), dma((3,)), dma((3,)), dma((4, 3)), dma((4, 3)),
        ],
        compiler_params=pltpu.CompilerParams(
            collective_id=0, has_side_effects=True, vmem_limit_bytes=52 * 1024 * 1024
        ),
    )(*(pltpu.with_memory_space_constraint(a, pltpu.HBM) for a in (stack, codes, valid_mask[0])))
    out = pl.pallas_call(
        write_out,
        out_shape=[jax.ShapeDtypeStruct((n, ROWS, cols), f32) for n in (2, 3, 7)],
        in_specs=[pl.BlockSpec(memory_space=pl.ANY)],
        out_specs=[hbm] * 3,
        scratch_shapes=[dma((3,))],
        compiler_params=pltpu.CompilerParams(vmem_limit_bytes=1024 * 1024),
    )(maps)
    return tuple(one[:, None] for one in out)


def solution(mesh):
    in_specs = (
        P("layer", "angle", "tile", None),
        P("layer", "angle", "tile", None),
        P("layer", "tile", "angle"),
    )
    out_specs = (
        P(None, "layer", "tile", "angle"),
        P(None, "layer", "tile", "angle"),
        P(None, "layer", "tile", "angle"),
    )
    return jax.shard_map(
        functools.partial(on_device, mesh.shape["angle"], mesh.shape["tile"]),
        mesh=mesh, in_specs=in_specs, out_specs=out_specs, check_vma=False,
    )
```

```python
import functools

import jax
import jax.numpy as jnp
from jax import lax
from jax.experimental import pallas as pl
from jax.experimental.pallas import tpu as pltpu
from jax.sharding import PartitionSpec as P

NPHI = 32
NCHI = 32
MOMENTS = 6
ROWS = 24
ANGLES_HERE = 128
LANES = 128
HALF = ANGLES_HERE // 2
DEPTH = HALF * 16
LAYER_PITCH = 2.0
AHEAD = 3
ORDER = (0, 2, 1)
MESH = pl.DeviceIdType.MESH


def fill_tables(me, spread_ref, weight_ref):
    lane = lax.broadcasted_iota(jnp.int32, (ANGLES_HERE, DEPTH), 1)
    source = lax.broadcasted_iota(jnp.int32, (ANGLES_HERE, DEPTH), 0)
    pair = lane >> 4
    for parity in range(2):
        hit = source == 2 * pair + parity
        spread_ref[parity * ANGLES_HERE : (parity + 1) * ANGLES_HERE, :] = jnp.where(
            hit, 1.0, 0.0
        ).astype(jnp.bfloat16)
    lane = lax.broadcasted_iota(jnp.int32, (16, DEPTH), 1)
    row = lax.broadcasted_iota(jnp.int32, (16, DEPTH), 0)
    inner = lane & 15
    keep = inner == row
    for kind in range(3):
        if kind == 0:
            parity = 0
        elif kind == 2:
            parity = 1
        else:
            parity = inner >> 3
        angle = me * ANGLES_HERE + 2 * (lane >> 4) + parity
        phi = ((angle >> 5).astype(jnp.float32) - 0.5 * (NPHI - 1)) / (0.5 * NPHI)
        chi = ((angle & 31).astype(jnp.float32) - 0.5 * (NCHI - 1)) / (0.5 * NCHI)
        rows = (jnp.ones_like(phi), phi, chi, phi * phi, chi * chi, phi * chi)
        for m in range(MOMENTS):
            weight_ref[kind, m] = jnp.where(keep, rows[m], 0.0).astype(jnp.bfloat16)


def fill_factors(exp_ref, factor_ref):
    blank = jnp.zeros((8, ANGLES_HERE), jnp.float32)

    def one(k, carry):
        code = exp_ref[pl.ds(k, ROWS, stride=16), :]
        factor = jnp.exp2(code.astype(jnp.float32))
        low, mid, high = factor[0:8], factor[8:16], factor[16:24]
        even = jnp.concatenate([low, mid, high, blank, blank, blank], axis=0)
        odd = jnp.concatenate([blank, blank, blank, low, mid, high], axis=0)
        both = jnp.concatenate([even, odd], axis=1)
        factor_ref[k] = both.astype(jnp.bfloat16)
        return carry

    lax.fori_loop(0, 16, one, 0)


def grow(step, dest, factor_ref, spread_ref, grown_ref):
    both = factor_ref[pl.ds(2 * dest, 2)].reshape(96, 2 * ANGLES_HERE)
    grown_ref[lax.rem(step, 2)] = jnp.dot(
        both, spread_ref[...], preferred_element_type=jnp.float32
    ).astype(jnp.bfloat16)


def partial_moments(step, role, buf, grown_ref, weight_ref, part):
    slot = lax.rem(step, 2)
    for side in range(2):
        sums = []
        for kind in range(3):
            begin = side * 48 + kind * 16
            left = (weight_ref[kind] * grown_ref[slot, begin : begin + 16][None]).reshape(
                MOMENTS * 16, DEPTH
            )
            right = buf[
                role, :, kind * 16 : kind * 16 + 16, side * LANES : (side + 1) * LANES
            ].reshape(DEPTH, LANES)
            sums.append(
                jnp.dot(left, right, preferred_element_type=jnp.float32).reshape(
                    MOMENTS, 16, LANES
                )
            )
        first, second, third = sums
        here = slice(side * LANES, (side + 1) * LANES)
        part[role, :, 0:8, here] = first[:, 0:8] + second[:, 8:16]
        part[role, :, 8:16, here] = first[:, 8:16] + third[:, 0:8]
        part[role, :, 16:24, here] = second[:, 0:8] + third[:, 8:16]


def kernel(
    sizes, frames, exponents, valid, out,
    buf, exp_ref, mask_ref, factor_ref, spread_ref, weight_ref, grown_ref,
    part, early, far, late, last, orient,
    left_halo, right_halo, up_halo, down_halo, layer_halo,
    in_sem, small_sem, early_send, early_recv, far_send, far_recv,
    late_send, late_recv, last_send, last_recv, halo_send, halo_recv,
):
    count, tiles = sizes
    ring = count // 2
    me = lax.axis_index("angle")
    tile = lax.axis_index("tile")
    layer = lax.axis_index("layer")
    cols = 2 * LANES
    px, py = me // ring, lax.rem(me, ring)
    other = (1 - px) * ring + py
    above = px * ring + lax.rem(py + 1, ring)
    below = px * ring + lax.rem(py + ring - 1, ring)
    across = px * ring + lax.rem(py + 2, ring)
    has_next_tile = tile < tiles - 1
    has_last_tile = tile > 0
    has_next_angle = me < count - 1
    has_last_angle = me > 0
    far_next = me == ring - 1
    far_last = me == ring

    def owner(role):
        swap = jnp.logical_or(role < 3, role == 6)
        turn = lax.rem(role, 3)
        shift = jnp.where(role < 6, jnp.where(turn == 0, 2, jnp.where(turn == 1, 1, ring - 1)), 0)
        return jnp.where(swap, 1 - px, px) * ring + lax.rem(py + shift, ring)

    def role_at(step):
        return jnp.where(step < 2, 1 - step, step)

    def chunk(role):
        begin = pl.multiple_of(owner(role) * cols, cols)
        return pltpu.make_async_copy(
            frames.at[:, :, pl.ds(begin, cols)], buf.at[role], in_sem.at[role]
        )

    exp_copy = pltpu.make_async_copy(exponents, exp_ref, small_sem.at[0])
    mask_copy = pltpu.make_async_copy(valid, mask_ref, small_sem.at[1])
    exp_copy.start()
    for role in range(AHEAD):
        chunk(role_at(jnp.int32(role))).start()

    barrier = pltpu.get_barrier_semaphore()

    def greet(where):
        pl.semaphore_signal(barrier, inc=1, device_id=where, device_id_type=MESH)

    greet({"angle": other})
    greet({"angle": above})
    greet({"angle": below})
    greet({"angle": across})
    greet({"layer": 1 - layer})
    pl.when(has_last_tile)(lambda: greet({"tile": tile - 1}))
    pl.when(has_next_tile)(lambda: greet({"tile": tile + 1}))
    pl.when(far_next)(lambda: greet({"angle": me + 1}))
    pl.when(far_last)(lambda: greet({"angle": me - 1}))
    partners = 5
    for present in (has_last_tile, has_next_tile, far_next, far_last):
        partners = partners + present.astype(jnp.int32)

    fill_tables(me, spread_ref, weight_ref)
    exp_copy.wait()
    mask_copy.start()
    fill_factors(exp_ref, factor_ref)
    grow(jnp.int32(0), owner(role_at(jnp.int32(0))), factor_ref, spread_ref, grown_ref)

    def remote(src, dst, send, recv, where):
        return pltpu.make_async_remote_copy(
            src_ref=src, dst_ref=dst, send_sem=send, recv_sem=recv, device_id=where,
            device_id_type=MESH,
        )

    def rows(g):
        return pl.ds(8 * g, 8)

    def early_copy(role, g):
        to = jnp.where(role == 0, other, jnp.where(role == 1, above, below))
        return remote(
            part.at[role, :, rows(g), :], early.at[role, :, rows(g), :],
            early_send.at[role, g], early_recv.at[role, g], {"angle": to},
        )

    def far_copy(g):
        return remote(
            part.at[3, :, rows(g), :], far.at[:, rows(g), :], far_send.at[g], far_recv.at[g],
            {"angle": across},
        )

    def late_copy(side):
        return remote(
            part.at[4 + side], late.at[side], late_send.at[side], late_recv.at[side],
            {"angle": below if side else above},
        )

    def last_copy(g):
        return remote(
            part.at[6, :, rows(g), :], last.at[:, rows(g), :], last_send.at[g], last_recv.at[g],
            {"angle": other},
        )

    def one(step, carry):
        role = role_at(step)
        chunk(role).wait()

        @pl.when(step + AHEAD < count)
        def _():
            chunk(step + AHEAD).start()

        following = jnp.minimum(step + 1, count - 1)
        grow(step + 1, owner(role_at(following)), factor_ref, spread_ref, grown_ref)
        partial_moments(step, role, buf, grown_ref, weight_ref, part)

        @pl.when(step == 0)
        def _():
            pl.semaphore_wait(barrier, partners)

        @pl.when(role < 3)
        def _():
            for g in ORDER:
                early_copy(role, g).start()

        for side in range(2):

            @pl.when(role == 4 + side)
            def _():
                late_copy(side).start()

        for turn, g in enumerate(ORDER):

            @pl.when(step == 5 + turn)
            def _():
                here = slice(8 * g, 8 * g + 8)
                early_copy(0, g).wait_recv()
                part[3, :, here] += early[0, :, here]
                far_copy(g).start()

        return carry

    lax.fori_loop(0, count, one, 0)

    for g in ORDER:
        here = slice(8 * g, 8 * g + 8)
        early_copy(1, g).wait_recv()
        early_copy(2, g).wait_recv()
        part[6, :, here] += early[1, :, here] + early[2, :, here]
        last_copy(g).start()
    @pl.when(jnp.logical_not(has_last_tile))
    def _():
        up_halo[...] = jnp.zeros_like(up_halo)

    @pl.when(jnp.logical_not(has_next_tile))
    def _():
        down_halo[...] = jnp.zeros_like(down_halo)

    @pl.when(jnp.logical_not(has_last_angle))
    def _():
        left_halo[...] = jnp.zeros_like(left_halo)

    @pl.when(jnp.logical_not(has_next_angle))
    def _():
        right_halo[...] = jnp.zeros_like(right_halo)

    def to_layer(g):
        return remote(
            orient.at[:, rows(g), :], layer_halo.at[:, rows(g), :],
            halo_send.at[0, g], halo_recv.at[0, g], {"layer": 1 - layer},
        )

    def to_next_angle(g):
        return remote(
            orient.at[:, rows(g), LANES:cols], left_halo.at[:, rows(g), :],
            halo_send.at[1, g], halo_recv.at[1, g], {"angle": me + 1},
        )

    def to_last_angle(g):
        return remote(
            orient.at[:, rows(g), 0:LANES], right_halo.at[:, rows(g), :],
            halo_send.at[2, g], halo_recv.at[2, g], {"angle": me - 1},
        )

    to_next_tile = remote(
        orient.at[:, rows(2), :], up_halo, halo_send.at[3, 0], halo_recv.at[3, 0],
        {"tile": tile + 1},
    )
    to_last_tile = remote(
        orient.at[:, rows(0), :], down_halo, halo_send.at[3, 1], halo_recv.at[3, 1],
        {"tile": tile - 1},
    )

    for side in range(2):
        late_copy(side).wait_recv()
    for g in ORDER:
        here = slice(8 * g, 8 * g + 8)
        far_copy(g).wait_recv()
        last_copy(g).wait_recv()
        total = (part[7, :, here] + far[:, here]) + (late[0, :, here] + late[1, :, here])
        total = total + last[:, here]
        field = [total[1] / total[0], total[2] / total[0]]
        orient[0, here] = field[0]
        orient[1, here] = field[1]
        part[7, :, here] = total
        pl.when(has_next_angle)(lambda: to_next_angle(g).start())
        pl.when(has_last_angle)(lambda: to_last_angle(g).start())
        if g == 0:
            pl.when(has_last_tile)(lambda: to_last_tile.start())
        if g == 2:
            pl.when(has_next_tile)(lambda: to_next_tile.start())
        to_layer(g).start()
    mask_copy.wait()
    for g in ORDER:
        here = slice(8 * g, 8 * g + 8)
        mask = mask_ref[here].astype(jnp.float32)
        out[0, here] = orient[0, here] * mask
        out[1, here] = orient[1, here] * mask
        zeroth = part[7, 0, here]
        out[2, here] = (part[7, 3, here] / zeroth - orient[0, here] * orient[0, here]) * mask
        out[3, here] = (part[7, 4, here] / zeroth - orient[1, here] * orient[1, here]) * mask
        out[4, here] = (part[7, 5, here] / zeroth - orient[0, here] * orient[1, here]) * mask

    pl.when(has_last_tile)(lambda: to_next_tile.wait_recv())
    pl.when(has_next_tile)(lambda: to_last_tile.wait_recv())
    for g in ORDER:
        pl.when(has_last_angle)(lambda: to_next_angle(g).wait_recv())
        pl.when(has_next_angle)(lambda: to_last_angle(g).wait_recv())

    mask = mask_ref[...].astype(jnp.float32)
    lane = lax.broadcasted_iota(jnp.int32, (ROWS, cols), 1)
    row = lax.broadcasted_iota(jnp.int32, (ROWS, cols), 0)
    along_x, along_y = [], []
    for f in range(2):
        field = orient[f]
        after = jnp.where(
            lane == cols - 1, right_halo[f, :, 0:1], pltpu.roll(field, cols - 1, 1)
        )
        before = jnp.where(lane == 0, left_halo[f, :, LANES - 1 : LANES], pltpu.roll(field, 1, 1))
        along_x.append(0.5 * (after - before))
        after = jnp.where(row == ROWS - 1, down_halo[f, 0:1, :], pltpu.roll(field, ROWS - 1, 0))
        before = jnp.where(row == 0, up_halo[f, 7:8, :], pltpu.roll(field, 1, 0))
        along_y.append(0.5 * (after - before))
    out[5] = -along_y[1] * mask
    out[6] = -along_x[0] * mask
    out[7] = -(along_x[0] + along_y[1]) * mask
    out[8] = along_x[1] * mask
    out[9] = along_y[0] * mask
    for g in ORDER:
        to_layer(g).wait_recv()
    slope = (0.5 / LAYER_PITCH) * (1 - 2 * layer).astype(jnp.float32) * mask
    out[10] = layer_halo[0] * slope
    out[11] = layer_halo[1] * slope

    for g in ORDER:
        for role in range(3):
            early_copy(role, g).wait_send()
        far_copy(g).wait_send()
        last_copy(g).wait_send()
        to_layer(g).wait_send()
        pl.when(has_next_angle)(lambda: to_next_angle(g).wait_send())
        pl.when(has_last_angle)(lambda: to_last_angle(g).wait_send())
    for side in range(2):
        late_copy(side).wait_send()
    pl.when(has_next_tile)(lambda: to_next_tile.wait_send())
    pl.when(has_last_tile)(lambda: to_last_tile.wait_send())


def write_out(maps, orient_out, spread_out, nye_out, sem):
    copies = [
        pltpu.make_async_copy(maps.at[0:2], orient_out, sem.at[0]),
        pltpu.make_async_copy(maps.at[2:5], spread_out, sem.at[1]),
        pltpu.make_async_copy(maps.at[5:12], nye_out, sem.at[2]),
    ]
    for copy in copies:
        copy.start()
    for copy in copies:
        copy.wait()


def on_device(count, tiles, frames, exponents, valid_mask):
    columns = frames.shape[3]
    cols = columns // count
    stack = frames.reshape(HALF, 2 * ROWS, columns)
    codes = exponents[0].transpose(1, 2, 0).reshape(ROWS * 16, ANGLES_HERE)
    f32 = jnp.float32
    bf16 = jnp.bfloat16
    dma = pltpu.SemaphoreType.DMA
    hbm = pl.BlockSpec(memory_space=pltpu.HBM)
    vmem = pl.BlockSpec(memory_space=pltpu.VMEM)
    block = (MOMENTS, ROWS, cols)
    maps = pl.pallas_call(
        functools.partial(kernel, (count, tiles)),
        out_shape=jax.ShapeDtypeStruct((12, ROWS, cols), f32),
        in_specs=[pl.BlockSpec(memory_space=pl.ANY)] * 3,
        out_specs=vmem,
        scratch_shapes=[
            pltpu.VMEM((count, HALF, 2 * ROWS, cols), bf16),
            pltpu.VMEM((ROWS * 16, ANGLES_HERE), jnp.int32),
            pltpu.VMEM((ROWS, cols), jnp.int32),
            pltpu.VMEM((16, 48, 2 * ANGLES_HERE), bf16),
            pltpu.VMEM((2 * ANGLES_HERE, DEPTH), bf16),
            pltpu.VMEM((3, MOMENTS, 16, DEPTH), bf16),
            pltpu.VMEM((2, 96, DEPTH), bf16),
            pltpu.VMEM((count,) + block, f32),
            pltpu.VMEM((3,) + block, f32),
            pltpu.VMEM(block, f32),
            pltpu.VMEM((2,) + block, f32),
            pltpu.VMEM(block, f32),
            pltpu.VMEM((2, ROWS, cols), f32),
            pltpu.VMEM((2, ROWS, LANES), f32),
            pltpu.VMEM((2, ROWS, LANES), f32),
            pltpu.VMEM((2, 8, cols), f32),
            pltpu.VMEM((2, 8, cols), f32),
            pltpu.VMEM((2, ROWS, cols), f32),
            dma((count,)), dma((2,)), dma((3, 3)), dma((3, 3)), dma((3,)), dma((3,)),
            dma((2,)), dma((2,)), dma((3,)), dma((3,)), dma((4, 3)), dma((4, 3)),
        ],
        compiler_params=pltpu.CompilerParams(
            collective_id=0, has_side_effects=True, vmem_limit_bytes=52 * 1024 * 1024
        ),
    )(*(pltpu.with_memory_space_constraint(a, pltpu.HBM) for a in (stack, codes, valid_mask[0])))
    out = pl.pallas_call(
        write_out,
        out_shape=[jax.ShapeDtypeStruct((n, ROWS, cols), f32) for n in (2, 3, 7)],
        in_specs=[pl.BlockSpec(memory_space=pl.ANY)],
        out_specs=[hbm] * 3,
        scratch_shapes=[dma((3,))],
        compiler_params=pltpu.CompilerParams(vmem_limit_bytes=1024 * 1024),
    )(maps)
    return tuple(one[:, None] for one in out)


def solution(mesh):
    in_specs = (
        P("layer", "angle", "tile", None),
        P("layer", "angle", "tile", None),
        P("layer", "tile", "angle"),
    )
    out_specs = (
        P(None, "layer", "tile", "angle"),
        P(None, "layer", "tile", "angle"),
        P(None, "layer", "tile", "angle"),
    )
    return jax.shard_map(
        functools.partial(on_device, mesh.shape["angle"], mesh.shape["tile"]),
        mesh=mesh, in_specs=in_specs, out_specs=out_specs, check_vma=False,
    )
```
